32 devices in a mesh: dp: 2 (over x), seq: 2 (over core), expert: 8 (over z, y).
Axes of the slice: x: 2, y: 2, z: 4, core: 2. Of those that a mesh axis runs over, the one named last changes fastest.
Arguments:
- out_grad: bfloat16 [4096, 2048], P(('dp', 'seq', 'expert')), may hold values from -6 to 6
- saved_act: bfloat16 [4096, 8, 768], P(('dp', 'seq', 'expert')), may hold values from -0.29882812 to 0.29882812
- gate_probs: float32 [4096, 8], P(('dp', 'seq', 'expert')), may hold values from 0.02 to 0.6
- routes: int32 [4096, 8], P(('dp', 'seq', 'expert')), may hold values from 0 to 15, all different within a row; in each aligned block of 128 rows (0 to 127, 128 to 255, ...) at most 72 rows name the same one
- w_down: bfloat16 [16, 768, 2048], P(('seq', 'expert'), 'dp'), may hold values from -0.21875 to 0.21875
Outputs:
- act_grad: bfloat16 [4096, 8, 768], P(('dp', 'seq', 'expert'))
- prob_grad: float32 [4096, 8], P(('dp', 'seq', 'expert'))
- weight_grad: bfloat16 [16, 768, 2048], P(('seq', 'expert'), 'dp')
The draws below stay inside these ranges and needn't reach their ends.
Inputs may be any that keep to these rules, and one draw needn't show every extreme that they name: `routes`: within the rows of one device (aligned blocks of 128 tokens) no expert is named by more than 72 tokens, a bound that some block reaches; each token names 8 different experts.
All inputs are finite; a program needn't handle non-finite values.
Results may differ from the reference program's by a relative error of at most 0.014.
Values may be sent and summed in bfloat16 or wider, within the bound.
A program may use at most 128 MiB of HBM per device.

```python
import math
import jax
import jax.numpy as jnp
import numpy as np
from jax import lax

D = 2048
FF = 768
TOPK = 8
TOK_DEV = 128
EXPERTS = 16
TOKENS = 4096
MOST = 72
N_DP = 2
N_SEQ = 2
N_EXPERT = 8


def shard_levels(stream_key, shape, shards, low, largest):
    loudness = 1.0
    for dim, parts in shards:
        draws = jax.random.uniform(jax.random.fold_in(jax.random.fold_in(stream_key, 6), dim), (parts,), jnp.float32, low / len(shards), largest / len(shards))
        loudness = loudness * jnp.repeat(jnp.exp(draws), shape[dim] // parts).reshape((-1,) + (1,) * (len(shape) - 1 - dim))
    return loudness


def shared_out(rng, own, number, rows, amount, top, bound, slope):
    sequence = jax.random.permutation(rng, amount)
    heavy_load, ordinary = shares(amount, rows * top, bound, slope, True), shares(amount, rows * top, bound, slope, False)
    places = jnp.arange(amount)

    def named(tallies, rotation):
        used = int((tallies > 0).sum())
        fixed = max(1, used // 4)
        passed = fixed + (places - fixed + rotation * (used - fixed)) % max(1, amount - fixed)
        return jnp.zeros((amount,), jnp.int32).at[sequence[jnp.where(places < fixed, places, passed)]].set(jnp.asarray(tallies, jnp.int32))

    tallies = jnp.where(number % 4 == 0, named(heavy_load, number // 4), named(ordinary, number - number // 4 - 1))
    mixed = jax.random.permutation(jax.random.fold_in(own, 3), amount)
    giver, taker = mixed[0:amount // 2 * 2:2], mixed[1:amount // 2 * 2:2]
    margin = jnp.minimum(tallies[giver] - 1, bound - tallies[taker]) // 2
    margin = jnp.where((giver == sequence[0]) | (taker == sequence[0]) | (tallies[taker] == 0), 0, jnp.maximum(margin, 0))
    passed = jax.random.randint(jax.random.fold_in(own, 4), (amount // 2,), 0, 1 << 20) % (margin + 1)
    tallies = tallies.at[giver].add(-passed).at[taker].add(passed)
    members = jnp.searchsorted(jnp.cumsum(tallies), jnp.arange(rows * top), side="right").astype(jnp.int32)
    grid = members.reshape(top, rows).T
    grid = grid[jax.random.permutation(jax.random.fold_in(own, 1), rows)]
    rotation = jax.random.randint(jax.random.fold_in(own, 2), (rows, 1), 0, top)
    return jnp.take_along_axis(grid, (jnp.arange(top)[None, :] + rotation) % top, axis=1)


def shares(count, total, bound, skew, full):
    portions = [(1 << 20) // math.isqrt(standing ** skew) + 1 for standing in range(1, count + 1)]
    largest = bound if full else min(bound, max(-(-total // count), total * portions[0] // sum(portions)))
    least = 1 if total - largest >= count - 1 else 0
    given, spare = [largest] + [least] * (count - 1), total - largest - least * (count - 1)
    while spare > 0:
        free = [i for i in range(1, count) if given[i] < largest] or [i for i in range(1, count) if given[i] < bound]
        pool, remaining = sum([portions[i] for i in free]), spare
        for i in free:
            addition = min(bound - given[i], max(1, remaining * portions[i] // pool), spare)
            given[i] = given[i] + addition
            spare = spare - addition
    return np.array(given)


def normal_values(stream_key, extent, scale, most, shards=(), kind=jnp.bfloat16):
    drawn = jax.random.normal(stream_key, extent, jnp.float32) * scale
    if len(shards) > 0:
        drawn = shard_levels(stream_key, extent, shards, -0.22, 0.18) * drawn
    return jnp.clip(drawn, min=-most, max=most).astype(kind)


def setup_inputs(seed: int = 0) -> dict:
    streams_of = jax.random.split(jax.random.key(seed), 6)
    out_grad = normal_values(streams_of[0], (TOKENS, D), 1.0, 6.0, ((0, 32),))
    saved_act = normal_values(streams_of[1], (TOKENS, TOPK, FF), 0.05, 0.29882812, ((0, 32),))
    gate_probs = jnp.clip(jnp.exp(math.log(0.6) - 3.4011974 * jax.random.uniform(streams_of[2], (TOKENS, TOPK), jnp.float32) ** shard_levels(streams_of[2], (TOKENS, TOPK), ((0, 32),), -0.2, 0.2)), 0.02, 0.6)
    routes_keys = jax.random.split(jax.random.fold_in(streams_of[3], 1), TOKENS // TOK_DEV)
    routes_turns = jax.random.permutation(jax.random.fold_in(streams_of[3], 3), TOKENS // TOK_DEV)
    routes = jax.vmap(lambda own, number: shared_out(jax.random.fold_in(streams_of[3], 2), own, number, TOK_DEV, EXPERTS, TOPK, MOST, 2))(routes_keys, routes_turns).reshape((TOKENS, TOPK))
    w_down = normal_values(streams_of[4], (EXPERTS, FF, D), FF ** -0.5, 0.21875, ((0, 16), (1, 2)))
    return dict(out_grad=out_grad, saved_act=saved_act, gate_probs=gate_probs, routes=routes, w_down=w_down)


def reference(out_grad, saved_act, gate_probs, routes, w_down):
    tok_group = TOKENS // N_DP
    rows_group = tok_group * TOPK
    slot_total = N_SEQ * N_EXPERT * MOST
    weight_all = w_down.astype(jnp.float32)
    weight_sum = jnp.zeros((EXPERTS, FF, D), jnp.float32)
    grad_parts = []
    prob_parts = []
    lane_ids = jnp.arange(slot_total, dtype=jnp.int32)
    for group_index in range(N_DP):
        first = group_index * tok_group
        group_out = out_grad[first:first + tok_group].astype(jnp.float32)
        group_act = saved_act[first:first + tok_group].reshape(rows_group, FF).astype(jnp.float32)
        group_prob = gate_probs[first:first + tok_group].reshape(rows_group)
        group_route = routes[first:first + tok_group].reshape(rows_group).astype(jnp.int32)
        sorted_rows = jnp.argsort(group_route, stable=True).astype(jnp.int32)
        counts = jax.ops.segment_sum(jnp.ones((rows_group,), jnp.int32), group_route, num_segments=EXPERTS)
        starts = (jnp.cumsum(counts) - counts).astype(jnp.int32)

        def per_expert(expert):
            is_live = lane_ids < counts[expert]
            row_ids = sorted_rows[jnp.minimum(starts[expert] + lane_ids, rows_group - 1)]
            grad_in = group_out[row_ids // TOPK]
            act_in = group_act[row_ids]
            prob_in = jnp.where(is_live, group_prob[row_ids], jnp.zeros((), jnp.float32))
            weight_one = lax.dynamic_index_in_dim(weight_all, expert, 0, keepdims=False)
            grad_rows = jnp.dot(grad_in, weight_one.T, precision=lax.Precision.HIGHEST)
            act_out = (prob_in[:, None] * grad_rows).astype(jnp.bfloat16)
            prob_out = jnp.sum(act_in * grad_rows, axis=1)
            scaled_low = (prob_in[:, None] * grad_in).astype(jnp.bfloat16)
            scaled = lax.optimization_barrier(scaled_low).astype(jnp.float32)
            partial_value = jnp.dot(act_in.T, scaled, precision=lax.Precision.HIGHEST)
            partial_low = lax.optimization_barrier(partial_value.astype(jnp.bfloat16)).astype(jnp.float32)
            target = jnp.where(is_live, row_ids, rows_group)
            return act_out, prob_out, partial_low, target

        act_out, prob_out, partial_low, target = lax.map(per_expert, jnp.arange(EXPERTS, dtype=jnp.int32))
        flat_target = target.reshape(-1)
        grad_flat = jnp.zeros((rows_group, FF), jnp.bfloat16).at[flat_target].set(act_out.reshape(-1, FF).astype(jnp.bfloat16), mode="drop")
        prob_flat = jnp.zeros((rows_group,), jnp.float32).at[flat_target].set(prob_out.reshape(-1), mode="drop")
        grad_parts.append(grad_flat.reshape(tok_group, TOPK, FF))
        prob_parts.append(prob_flat.reshape(tok_group, TOPK))
        weight_sum = weight_sum + partial_low
    act_grad = jnp.concatenate(grad_parts, axis=0)
    prob_grad = jnp.concatenate(prob_parts, axis=0)
    return act_grad, prob_grad, weight_sum.astype(jnp.bfloat16)
```

```python
import jax
import jax.numpy as jnp
from jax import lax
from jax.sharding import PartitionSpec as P

GROUP = ("seq", "expert")


def local(out_grad, saved_act, gate_probs, routes, w_down):
    tokens, top = routes.shape
    hidden = saved_act.shape[2]
    features = out_grad.shape[1]
    owners = lax.axis_size(GROUP)
    pairs = tokens * top
    most = max(2, min(tokens, pairs // owners + pairs // (8 * owners)))
    rows = -(-most // 8) * 8
    capacity = owners * rows
    f32, bf16 = jnp.float32, jnp.bfloat16

    grads_all = lax.all_gather(out_grad, GROUP, axis=0)
    routes_all = lax.all_gather(routes, GROUP, axis=0)
    weight = lax.all_gather(w_down, "dp", axis=1, tiled=True)[0]

    ids = jnp.arange(owners, dtype=jnp.int32)
    named = routes[:, :, None] == ids[None, None, :]
    names = jnp.any(named, axis=1)
    before = (jnp.arange(tokens)[:, None] > jnp.arange(tokens)[None, :]).astype(bf16)
    rank = jnp.dot(before, names.astype(bf16), preferred_element_type=f32)
    rank_of = jnp.sum(jnp.where(named, rank[:, None, :], 0.0), axis=2).astype(jnp.int32)
    slot = (routes * rows + rank_of).reshape(pairs)
    place = (slot[:, None] == jnp.arange(capacity, dtype=jnp.int32)[None, :]).astype(bf16)

    act = saved_act.reshape(pairs, hidden)
    gate = gate_probs.reshape(pairs, 1)
    scaled = (act.astype(f32) * gate).astype(bf16)
    packed = lax.dot_general(
        place, scaled, (((0,), (0,)), ((), ())), preferred_element_type=f32
    ).astype(bf16)
    recv_act = lax.all_to_all(
        packed.reshape(owners, rows, hidden), GROUP, split_axis=0, concat_axis=0, tiled=True
    ).reshape(capacity, hidden)

    mine = lax.axis_index(GROUP)
    has = jnp.any(routes_all == mine, axis=2)
    rank_all = jnp.dot(has.astype(bf16), before.T, preferred_element_type=f32).astype(jnp.int32)
    pick = (
        has[:, None, :]
        & (rank_all[:, None, :] == jnp.arange(rows, dtype=jnp.int32)[None, :, None])
    ).astype(bf16)
    chosen = (
        lax.dot_general(pick, grads_all, (((2,), (1,)), ((0,), (0,))), preferred_element_type=f32)
        .astype(bf16)
        .reshape(capacity, features)
    )
    grad = lax.dot_general(
        chosen, weight, (((1,), (1,)), ((), ())), preferred_element_type=f32
    ).astype(bf16)
    back = lax.all_to_all(
        grad.reshape(owners, rows, hidden), GROUP, split_axis=0, concat_axis=0, tiled=True
    ).reshape(capacity, hidden)
    part = lax.dot_general(
        recv_act, chosen, (((0,), (0,)), ((), ())), preferred_element_type=f32
    ).astype(bf16)
    weight_grad = lax.psum_scatter(part, "dp", scatter_dimension=0, tiled=True).reshape(
        w_down.shape
    )
    home = jnp.dot(place, back, preferred_element_type=f32)
    act_grad = (home * gate).astype(bf16).reshape(saved_act.shape)
    prob_grad = jnp.sum(home * act.astype(f32), axis=1).reshape(routes.shape)
    return act_grad, prob_grad, weight_grad


def solution(mesh):
    in_specs = (
        P(("dp", "seq", "expert"), None),
        P(("dp", "seq", "expert"), None, None),
        P(("dp", "seq", "expert"), None),
        P(("dp", "seq", "expert"), None),
        P(("seq", "expert"), "dp", None),
    )
    out_specs = (
        P(("dp", "seq", "expert"), None, None),
        P(("dp", "seq", "expert"), None),
        P(("seq", "expert"), "dp", None),
    )
    return jax.shard_map(local, mesh=mesh, in_specs=in_specs, out_specs=out_specs, check_vma=False)
```

```python
import functools

import jax
import jax.numpy as jnp
from jax import lax
from jax.experimental import pallas as pl
from jax.experimental.pallas import tpu as pltpu
from jax.sharding import PartitionSpec as P

GROUP = ("seq", "expert")


def both(*tests):
    result = tests[0]
    for test in tests[1:]:
        result = jnp.logical_and(result, test)
    return result


def gather_kernel(sizes, own, weight, every, weights, here, zs, zr, ys, yr, cs, cr, ws, wr):
    n_dp, n_seq, n_expert, minor = sizes
    lines = n_expert // minor
    dp, seq, expert = lax.axis_index("dp"), lax.axis_index("seq"), lax.axis_index("expert")
    z, y = expert // minor, expert % minor

    def inside(value, size):
        return both(value >= 0, value < size)

    peers = [((lax.rem(dp + i, n_dp), seq, expert), None) for i in range(1, n_dp)]
    peers += [((dp, lax.rem(seq + i, n_seq), expert), None) for i in range(1, n_seq)]
    for way in (1, -1):
        peers.append(((dp, seq, expert + way * minor), inside(z + way, lines)))
        peers.append(((dp, seq, expert + way), inside(y + way, minor)))
    barrier = pltpu.get_barrier_semaphore()

    def when(test, body):
        if test is None:
            body()
        else:
            pl.when(test)(body)

    for device, test in peers:
        when(
            test,
            lambda device=device: pl.semaphore_signal(
                barrier, inc=1, device_id=device, device_id_type=pl.DeviceIdType.MESH
            ),
        )
    count = sum(1 if test is None else test.astype(jnp.int32) for _, test in peers)
    pl.semaphore_wait(barrier, count)

    sends = []

    def copy(source, target, send, recv, device):
        return pltpu.make_async_remote_copy(
            src_ref=source,
            dst_ref=target,
            send_sem=send,
            recv_sem=recv,
            device_id=device,
            device_id_type=pl.DeviceIdType.MESH,
        )

    def start(test, make):
        when(test, lambda: make().start())
        sends.append((test, make))

    def place(zb, yb):
        return seq * n_expert + zb * minor + yb

    def block(zb, yb, is_own):
        return own if is_own else every.at[place(zb, yb)]

    def z_copy(way, hop):
        zb = z - way * (hop - 1)
        return copy(
            block(zb, y, hop == 1),
            every.at[place(zb, y)],
            zs.at[(1 - way) // 2, hop],
            zr.at[(1 - way) // 2, hop],
            (dp, seq, expert + way * minor),
        )

    def y_copy(way, hop, zb, is_own):
        yb = y - way * (hop - 1)
        return copy(
            block(zb, yb, is_own and hop == 1),
            every.at[place(zb, yb)],
            ys.at[(1 - way) // 2, hop, zb],
            yr.at[(1 - way) // 2, hop, zb],
            (dp, seq, expert + way),
        )

    def c_copy(i, zb, yb, is_own):
        return copy(
            block(zb, yb, is_own),
            every.at[place(zb, yb)],
            cs.at[i, zb * minor + yb],
            cr.at[i, zb * minor + yb],
            (dp, lax.rem(seq + i, n_seq), expert),
        )

    def w_copy(i):
        return copy(
            weight, weights.at[dp], ws.at[i], wr.at[i], (lax.rem(dp + i, n_dp), seq, expert)
        )

    def landed(test, ref, sem):
        when(test, lambda: copy(ref, ref, sem, sem, (dp, seq, expert)).wait_recv())

    def to_cores(test, zb, yb, is_own):
        for i in range(1, n_seq):
            start(test, functools.partial(c_copy, i, zb, yb, is_own))

    def spread(test, zb, is_own):
        for way in (1, -1):
            go = inside(y + way, minor)
            go = go if test is None else both(test, go)
            start(go, functools.partial(y_copy, way, 1, zb, is_own))
        to_cores(test, zb, y, is_own)

    def arrive_y(test, zb):
        for hop in range(1, minor):
            for way in (1, -1):
                yb = y - way * hop
                got = inside(yb, minor)
                got = got if test is None else both(test, got)
                landed(got, every.at[place(zb, yb)], yr.at[(1 - way) // 2, hop, zb])
                if hop + 1 < minor:
                    start(
                        both(got, inside(y + way, minor)),
                        functools.partial(y_copy, way, hop + 1, zb, False),
                    )
                to_cores(got, zb, yb, False)

    for way in (1, -1):
        start(inside(z + way, lines), functools.partial(z_copy, way, 1))
    spread(None, z, True)
    for i in range(1, n_dp):
        start(None, functools.partial(w_copy, i))
    locals_ = [
        pltpu.make_async_copy(own, every.at[place(z, y)], here.at[0]),
        pltpu.make_async_copy(weight, weights.at[dp], here.at[1]),
    ]
    for one in locals_:
        one.start()
    waiting = [(None, z)]
    for hop in range(1, lines):
        fresh = []
        for way in (1, -1):
            zb = z - way * hop
            got = inside(zb, lines)
            landed(got, every.at[place(zb, y)], zr.at[(1 - way) // 2, hop])
            if hop + 1 < lines:
                start(both(got, inside(z + way, lines)), functools.partial(z_copy, way, hop + 1))
            spread(got, zb, False)
            fresh.append((got, zb))
        for test, zb in waiting:
            arrive_y(test, zb)
        waiting = fresh
    for test, zb in waiting:
        arrive_y(test, zb)
    for i in range(1, n_seq):
        other = lax.rem(seq - i + n_seq, n_seq)
        for e in range(n_expert):
            landed(None, every.at[other * n_expert + e], cr.at[i, e])
    for i in range(1, n_dp):
        landed(None, weights.at[lax.rem(dp - i + n_dp, n_dp)], wr.at[i])
    for test, make in sends:
        when(test, lambda make=make: make().wait_send())
    for one in locals_:
        one.wait()


def gather(out_grad, weight):
    n_dp, n_seq, n_expert = (lax.axis_size(name) for name in ("dp", "seq", "expert"))
    minor = 1 << ((n_expert.bit_length() - 1) // 2)
    lines = n_expert // minor
    sems = pltpu.SemaphoreType.DMA
    hbm = pl.BlockSpec(memory_space=pl.ANY)
    return pl.pallas_call(
        functools.partial(gather_kernel, (n_dp, n_seq, n_expert, minor)),
        out_shape=(
            jax.ShapeDtypeStruct((n_seq * n_expert,) + out_grad.shape, out_grad.dtype),
            jax.ShapeDtypeStruct((n_dp,) + weight.shape, weight.dtype),
        ),
        in_specs=[hbm, hbm],
        out_specs=(hbm, hbm),
        scratch_shapes=[
            sems((2,)),
            sems((2, lines)),
            sems((2, lines)),
            sems((2, minor, lines)),
            sems((2, minor, lines)),
            sems((n_seq, n_expert)),
            sems((n_seq, n_expert)),
            sems((n_dp,)),
            sems((n_dp,)),
        ],
        compiler_params=pltpu.CompilerParams(collective_id=0, has_side_effects=True),
        name="gather",
    )(out_grad, weight)


def local(out_grad, saved_act, gate_probs, routes, w_down):
    tokens, top = routes.shape
    hidden = saved_act.shape[2]
    features = out_grad.shape[1]
    owners = lax.axis_size(GROUP)
    pairs = tokens * top
    most = max(2, min(tokens, pairs // owners + pairs // (8 * owners)))
    rows = -(-most // 8) * 8
    capacity = owners * rows
    f32, bf16 = jnp.float32, jnp.bfloat16

    grads_all, weight = gather(out_grad, w_down[0])
    weight = weight.reshape(-1, features)
    routes_all = lax.all_gather(routes, GROUP, axis=0)

    ids = jnp.arange(owners, dtype=jnp.int32)
    named = routes[:, :, None] == ids[None, None, :]
    names = jnp.any(named, axis=1)
    before = (jnp.arange(tokens)[:, None] > jnp.arange(tokens)[None, :]).astype(bf16)
    rank = jnp.dot(before, names.astype(bf16), preferred_element_type=f32)
    rank_of = jnp.sum(jnp.where(named, rank[:, None, :], 0.0), axis=2).astype(jnp.int32)
    slot = (routes * rows + rank_of).reshape(pairs)
    place = (slot[:, None] == jnp.arange(capacity, dtype=jnp.int32)[None, :]).astype(bf16)

    act = saved_act.reshape(pairs, hidden)
    gate = gate_probs.reshape(pairs, 1)
    scaled = (act.astype(f32) * gate).astype(bf16)
    packed = lax.dot_general(
        place, scaled, (((0,), (0,)), ((), ())), preferred_element_type=f32
    ).astype(bf16)
    recv_act = lax.all_to_all(
        packed.reshape(owners, rows, hidden), GROUP, split_axis=0, concat_axis=0, tiled=True
    ).reshape(capacity, hidden)

    mine = lax.axis_index(GROUP)
    has = jnp.any(routes_all == mine, axis=2)
    rank_all = jnp.dot(has.astype(bf16), before.T, preferred_element_type=f32).astype(jnp.int32)
    pick = (
        has[:, None, :]
        & (rank_all[:, None, :] == jnp.arange(rows, dtype=jnp.int32)[None, :, None])
    ).astype(bf16)
    chosen = (
        lax.dot_general(pick, grads_all, (((2,), (1,)), ((0,), (0,))), preferred_element_type=f32)
        .astype(bf16)
        .reshape(capacity, features)
    )
    grad = lax.dot_general(
        chosen, weight, (((1,), (1,)), ((), ())), preferred_element_type=f32
    ).astype(bf16)
    back = lax.all_to_all(
        grad.reshape(owners, rows, hidden), GROUP, split_axis=0, concat_axis=0, tiled=True
    ).reshape(capacity, hidden)
    part = lax.dot_general(
        recv_act, chosen, (((0,), (0,)), ((), ())), preferred_element_type=f32
    ).astype(bf16)
    weight_grad = lax.psum_scatter(part, "dp", scatter_dimension=0, tiled=True).reshape(
        w_down.shape
    )
    home = jnp.dot(place, back, preferred_element_type=f32)
    act_grad = (home * gate).astype(bf16).reshape(saved_act.shape)
    prob_grad = jnp.sum(home * act.astype(f32), axis=1).reshape(routes.shape)
    return act_grad, prob_grad, weight_grad


def solution(mesh):
    in_specs = (
        P(("dp", "seq", "expert"), None),
        P(("dp", "seq", "expert"), None, None),
        P(("dp", "seq", "expert"), None),
        P(("dp", "seq", "expert"), None),
        P(("seq", "expert"), "dp", None),
    )
    out_specs = (
        P(("dp", "seq", "expert"), None, None),
        P(("dp", "seq", "expert"), None),
        P(("seq", "expert"), "dp", None),
    )
    return jax.shard_map(local, mesh=mesh, in_specs=in_specs, out_specs=out_specs, check_vma=False)
```

```python
import functools

import jax
import jax.numpy as jnp
from jax import lax
from jax.experimental import pallas as pl
from jax.experimental.pallas import tpu as pltpu
from jax.sharding import PartitionSpec as P

GROUP = ("seq", "expert")


def both(*tests):
    result = tests[0]
    for test in tests[1:]:
        result = jnp.logical_and(result, test)
    return result


def gather_kernel(
    sizes, own, weight, named, every, weights, names, here, zs, zr, ys, yr, cs, cr, ws, wr, rs, rr
):
    n_dp, n_seq, n_expert, minor = sizes
    lines = n_expert // minor
    dp, seq, expert = lax.axis_index("dp"), lax.axis_index("seq"), lax.axis_index("expert")
    z, y = expert // minor, expert % minor

    def inside(value, size):
        return both(value >= 0, value < size)

    n_group = n_seq * n_expert
    me = seq * n_expert + expert
    barrier = pltpu.get_barrier_semaphore()

    def member(i):
        index = lax.rem(me + i, n_group)
        return (dp, index // n_expert, lax.rem(index, n_expert))

    def greet(device):
        pl.semaphore_signal(
            barrier, inc=1, device_id=device, device_id_type=pl.DeviceIdType.MESH
        )

    lax.fori_loop(1, n_group, lambda i, _: greet(member(i)), None)
    for i in range(1, n_dp):
        greet((lax.rem(dp + i, n_dp), seq, expert))
    pl.semaphore_wait(barrier, n_group + n_dp - 2)

    def when(test, body):
        if test is None:
            body()
        else:
            pl.when(test)(body)

    sends = []

    def copy(source, target, send, recv, device):
        return pltpu.make_async_remote_copy(
            src_ref=source,
            dst_ref=target,
            send_sem=send,
            recv_sem=recv,
            device_id=device,
            device_id_type=pl.DeviceIdType.MESH,
        )

    def start(test, make):
        when(test, lambda: make().start())
        sends.append((test, make))

    def place(zb, yb):
        return seq * n_expert + zb * minor + yb

    def block(zb, yb, is_own):
        return own if is_own else every.at[place(zb, yb)]

    def z_copy(way, hop):
        zb = z - way * (hop - 1)
        return copy(
            block(zb, y, hop == 1),
            every.at[place(zb, y)],
            zs.at[(1 - way) // 2, hop],
            zr.at[(1 - way) // 2, hop],
            (dp, seq, expert + way * minor),
        )

    def y_copy(way, hop, zb, is_own):
        yb = y - way * (hop - 1)
        return copy(
            block(zb, yb, is_own and hop == 1),
            every.at[place(zb, yb)],
            ys.at[(1 - way) // 2, hop, zb],
            yr.at[(1 - way) // 2, hop, zb],
            (dp, seq, expert + way),
        )

    def c_copy(i, zb, yb, is_own):
        return copy(
            block(zb, yb, is_own),
            every.at[place(zb, yb)],
            cs.at[i, zb * minor + yb],
            cr.at[i, zb * minor + yb],
            (dp, lax.rem(seq + i, n_seq), expert),
        )

    def w_copy(i):
        return copy(
            weight, weights.at[dp], ws.at[i], wr.at[i], (lax.rem(dp + i, n_dp), seq, expert)
        )

    def landed(test, ref, sem):
        when(test, lambda: copy(ref, ref, sem, sem, (dp, seq, expert)).wait_recv())

    def to_cores(test, zb, yb, is_own):
        for i in range(1, n_seq):
            start(test, functools.partial(c_copy, i, zb, yb, is_own))

    def spread(test, zb, is_own):
        for way in (1, -1):
            go = inside(y + way, minor)
            go = go if test is None else both(test, go)
            start(go, functools.partial(y_copy, way, 1, zb, is_own))
        to_cores(test, zb, y, is_own)

    def arrive_y(test, zb):
        for hop in range(1, minor):
            for way in (1, -1):
                yb = y - way * hop
                got = inside(yb, minor)
                got = got if test is None else both(test, got)
                landed(got, every.at[place(zb, yb)], yr.at[(1 - way) // 2, hop, zb])
                if hop + 1 < minor:
                    start(
                        both(got, inside(y + way, minor)),
                        functools.partial(y_copy, way, hop + 1, zb, False),
                    )
                to_cores(got, zb, yb, False)

    def r_copy(i):
        return copy(named, names.at[me], rs.at[i], rr.at[i], member(i))

    for way in (1, -1):
        start(inside(z + way, lines), functools.partial(z_copy, way, 1))
    spread(None, z, True)
    for i in range(1, n_dp):
        start(None, functools.partial(w_copy, i))
    lax.fori_loop(1, n_group, lambda i, _: r_copy(i).start(), None)
    locals_ = [
        pltpu.make_async_copy(named, names.at[me], here.at[2]),
        pltpu.make_async_copy(own, every.at[place(z, y)], here.at[0]),
        pltpu.make_async_copy(weight, weights.at[dp], here.at[1]),
    ]
    for one in locals_:
        one.start()
    waiting = [(None, z)]
    for hop in range(1, lines):
        fresh = []
        for way in (1, -1):
            zb = z - way * hop
            got = inside(zb, lines)
            landed(got, every.at[place(zb, y)], zr.at[(1 - way) // 2, hop])
            if hop + 1 < lines:
                start(both(got, inside(z + way, lines)), functools.partial(z_copy, way, hop + 1))
            spread(got, zb, False)
            fresh.append((got, zb))
        for test, zb in waiting:
            arrive_y(test, zb)
        waiting = fresh
    for test, zb in waiting:
        arrive_y(test, zb)
    for i in range(1, n_seq):
        other = lax.rem(seq - i + n_seq, n_seq)
        for e in range(n_expert):
            landed(None, every.at[other * n_expert + e], cr.at[i, e])
    for i in range(1, n_dp):
        landed(None, weights.at[lax.rem(dp - i + n_dp, n_dp)], wr.at[i])

    def finish(i, _):
        landed(None, names.at[lax.rem(me - i + n_group, n_group)], rr.at[i])
        r_copy(i).wait_send()

    lax.fori_loop(1, n_group, finish, None)
    for test, make in sends:
        when(test, lambda make=make: make().wait_send())
    for one in locals_:
        one.wait()


def gather(out_grad, weight, named):
    n_dp, n_seq, n_expert = (lax.axis_size(name) for name in ("dp", "seq", "expert"))
    minor = 1 << ((n_expert.bit_length() - 1) // 2)
    lines = n_expert // minor
    sems = pltpu.SemaphoreType.DMA
    hbm = pl.BlockSpec(memory_space=pl.ANY)
    return pl.pallas_call(
        functools.partial(gather_kernel, (n_dp, n_seq, n_expert, minor)),
        out_shape=(
            jax.ShapeDtypeStruct((n_seq * n_expert,) + out_grad.shape, out_grad.dtype),
            jax.ShapeDtypeStruct((n_dp,) + weight.shape, weight.dtype),
            jax.ShapeDtypeStruct((n_seq * n_expert,) + named.shape, named.dtype),
        ),
        in_specs=[hbm, hbm, hbm],
        out_specs=(hbm, hbm, hbm),
        scratch_shapes=[
            sems((3,)),
            sems((2, lines)),
            sems((2, lines)),
            sems((2, minor, lines)),
            sems((2, minor, lines)),
            sems((n_seq, n_expert)),
            sems((n_seq, n_expert)),
            sems((n_dp,)),
            sems((n_dp,)),
            sems((n_seq * n_expert,)),
            sems((n_seq * n_expert,)),
        ],
        compiler_params=pltpu.CompilerParams(collective_id=0, has_side_effects=True),
        name="gather",
    )(out_grad, weight, named)


def local(out_grad, saved_act, gate_probs, routes, w_down):
    tokens, top = routes.shape
    hidden = saved_act.shape[2]
    features = out_grad.shape[1]
    owners = lax.axis_size(GROUP)
    pairs = tokens * top
    most = max(2, min(tokens, pairs // owners + pairs // (8 * owners)))
    rows = -(-most // 8) * 8
    capacity = owners * rows
    f32, bf16 = jnp.float32, jnp.bfloat16

    grads_all, weight, routes_all = gather(out_grad, w_down[0], routes.T)
    weight = weight.reshape(-1, features)

    ids = jnp.arange(owners, dtype=jnp.int32)
    named = routes[:, :, None] == ids[None, None, :]
    names = jnp.any(named, axis=1)
    before = (jnp.arange(tokens)[:, None] > jnp.arange(tokens)[None, :]).astype(bf16)
    rank = jnp.dot(before, names.astype(bf16), preferred_element_type=f32)
    rank_of = jnp.sum(jnp.where(named, rank[:, None, :], 0.0), axis=2).astype(jnp.int32)
    slot = (routes * rows + rank_of).reshape(pairs)
    place = (slot[:, None] == jnp.arange(capacity, dtype=jnp.int32)[None, :]).astype(bf16)

    act = saved_act.reshape(pairs, hidden)
    gate = gate_probs.reshape(pairs, 1)
    scaled = (act.astype(f32) * gate).astype(bf16)
    packed = lax.dot_general(
        place, scaled, (((0,), (0,)), ((), ())), preferred_element_type=f32
    ).astype(bf16)
    packed, grads_all, routes_all = lax.optimization_barrier((packed, grads_all, routes_all))
    recv_act = lax.all_to_all(
        packed.reshape(owners, rows, hidden), GROUP, split_axis=0, concat_axis=0, tiled=True
    ).reshape(capacity, hidden)

    mine = lax.axis_index(GROUP)
    has = jnp.any(routes_all == mine, axis=1)
    rank_all = jnp.dot(has.astype(bf16), before.T, preferred_element_type=f32).astype(jnp.int32)
    pick = (
        has[:, None, :]
        & (rank_all[:, None, :] == jnp.arange(rows, dtype=jnp.int32)[None, :, None])
    ).astype(bf16)
    chosen = (
        lax.dot_general(pick, grads_all, (((2,), (1,)), ((0,), (0,))), preferred_element_type=f32)
        .astype(bf16)
        .reshape(capacity, features)
    )
    grad = lax.dot_general(
        chosen, weight, (((1,), (1,)), ((), ())), preferred_element_type=f32
    ).astype(bf16)
    back = lax.all_to_all(
        grad.reshape(owners, rows, hidden), GROUP, split_axis=0, concat_axis=0, tiled=True
    ).reshape(capacity, hidden)
    recv_act, _ = lax.optimization_barrier((recv_act, grad))
    part = lax.dot_general(
        recv_act, chosen, (((0,), (0,)), ((), ())), preferred_element_type=f32
    ).astype(bf16)
    weight_grad = lax.psum_scatter(part, "dp", scatter_dimension=0, tiled=True).reshape(
        w_down.shape
    )
    home = jnp.dot(place, back, preferred_element_type=f32)
    act_grad = (home * gate).astype(bf16).reshape(saved_act.shape)
    prob_grad = jnp.sum(home * act.astype(f32), axis=1).reshape(routes.shape)
    return act_grad, prob_grad, weight_grad


def solution(mesh):
    in_specs = (
        P(("dp", "seq", "expert"), None),
        P(("dp", "seq", "expert"), None, None),
        P(("dp", "seq", "expert"), None),
        P(("dp", "seq", "expert"), None),
        P(("seq", "expert"), "dp", None),
    )
    out_specs = (
        P(("dp", "seq", "expert"), None, None),
        P(("dp", "seq", "expert"), None),
        P(("seq", "expert"), "dp", None),
    )
    return jax.shard_map(local, mesh=mesh, in_specs=in_specs, out_specs=out_specs, check_vma=False)
```

```python
import functools

import jax
import jax.numpy as jnp
from jax import lax
from jax.experimental import pallas as pl
from jax.experimental.pallas import tpu as pltpu
from jax.sharding import PartitionSpec as P

GROUP = ("seq", "expert")


def both(*tests):
    result = tests[0]
    for test in tests[1:]:
        result = jnp.logical_and(result, test)
    return result


def gather_kernel(
    sizes, own, weight, named, packed, every, weights, names, acts,
    here, zs, zr, ys, yr, cs, cr, ws, wr, rs, rr, sa, ra
):
    n_dp, n_seq, n_expert, minor = sizes
    lines = n_expert // minor
    dp, seq, expert = lax.axis_index("dp"), lax.axis_index("seq"), lax.axis_index("expert")
    z, y = expert // minor, expert % minor

    def inside(value, size):
        return both(value >= 0, value < size)

    n_group = n_seq * n_expert
    me = seq * n_expert + expert
    barrier = pltpu.get_barrier_semaphore()

    def member(i):
        index = lax.rem(me + i, n_group)
        return (dp, index // n_expert, lax.rem(index, n_expert))

    def greet(device):
        pl.semaphore_signal(
            barrier, inc=1, device_id=device, device_id_type=pl.DeviceIdType.MESH
        )

    lax.fori_loop(1, n_group, lambda i, _: greet(member(i)), None)
    for i in range(1, n_dp):
        greet((lax.rem(dp + i, n_dp), seq, expert))
    pl.semaphore_wait(barrier, n_group + n_dp - 2)

    def when(test, body):
        if test is None:
            body()
        else:
            pl.when(test)(body)

    sends = []

    def copy(source, target, send, recv, device):
        return pltpu.make_async_remote_copy(
            src_ref=source,
            dst_ref=target,
            send_sem=send,
            recv_sem=recv,
            device_id=device,
            device_id_type=pl.DeviceIdType.MESH,
        )

    def start(test, make):
        when(test, lambda: make().start())
        sends.append((test, make))

    def place(zb, yb):
        return seq * n_expert + zb * minor + yb

    def block(zb, yb, is_own):
        return own if is_own else every.at[place(zb, yb)]

    def z_copy(way, hop):
        zb = z - way * (hop - 1)
        return copy(
            block(zb, y, hop == 1),
            every.at[place(zb, y)],
            zs.at[(1 - way) // 2, hop],
            zr.at[(1 - way) // 2, hop],
            (dp, seq, expert + way * minor),
        )

    def y_copy(way, hop, zb, is_own):
        yb = y - way * (hop - 1)
        return copy(
            block(zb, yb, is_own and hop == 1),
            every.at[place(zb, yb)],
            ys.at[(1 - way) // 2, hop, zb],
            yr.at[(1 - way) // 2, hop, zb],
            (dp, seq, expert + way),
        )

    def c_copy(i, zb, yb, is_own):
        return copy(
            block(zb, yb, is_own),
            every.at[place(zb, yb)],
            cs.at[i, zb * minor + yb],
            cr.at[i, zb * minor + yb],
            (dp, lax.rem(seq + i, n_seq), expert),
        )

    def w_copy(i):
        return copy(
            weight, weights.at[dp], ws.at[i], wr.at[i], (lax.rem(dp + i, n_dp), seq, expert)
        )

    def landed(test, ref, sem):
        when(test, lambda: copy(ref, ref, sem, sem, (dp, seq, expert)).wait_recv())

    def to_cores(test, zb, yb, is_own):
        for i in range(1, n_seq):
            start(test, functools.partial(c_copy, i, zb, yb, is_own))

    def spread(test, zb, is_own):
        for way in (1, -1):
            go = inside(y + way, minor)
            go = go if test is None else both(test, go)
            start(go, functools.partial(y_copy, way, 1, zb, is_own))
        to_cores(test, zb, y, is_own)

    def arrive_y(test, zb):
        for hop in range(1, minor):
            for way in (1, -1):
                yb = y - way * hop
                got = inside(yb, minor)
                got = got if test is None else both(test, got)
                landed(got, every.at[place(zb, yb)], yr.at[(1 - way) // 2, hop, zb])
                if hop + 1 < minor:
                    start(
                        both(got, inside(y + way, minor)),
                        functools.partial(y_copy, way, hop + 1, zb, False),
                    )
                to_cores(got, zb, yb, False)

    def r_copy(i):
        return copy(named, names.at[me], rs.at[i], rr.at[i], member(i))

    def a_copy(i):
        index = lax.rem(me + i, n_group)
        return copy(packed.at[index], acts.at[me], sa.at[i], ra.at[i], member(i))

    for way in (1, -1):
        start(inside(z + way, lines), functools.partial(z_copy, way, 1))
    spread(None, z, True)
    for i in range(1, n_dp):
        start(None, functools.partial(w_copy, i))
    lax.fori_loop(1, n_group, lambda i, _: r_copy(i).start(), None)
    locals_ = [
        pltpu.make_async_copy(named, names.at[me], here.at[2]),
        pltpu.make_async_copy(packed.at[me], acts.at[me], here.at[3]),
        pltpu.make_async_copy(own, every.at[place(z, y)], here.at[0]),
        pltpu.make_async_copy(weight, weights.at[dp], here.at[1]),
    ]
    for one in locals_:
        one.start()
    waiting = [(None, z)]
    for hop in range(1, lines):
        fresh = []
        for way in (1, -1):
            zb = z - way * hop
            got = inside(zb, lines)
            landed(got, every.at[place(zb, y)], zr.at[(1 - way) // 2, hop])
            if hop + 1 < lines:
                start(both(got, inside(z + way, lines)), functools.partial(z_copy, way, hop + 1))
            spread(got, zb, False)
            fresh.append((got, zb))
        for test, zb in waiting:
            arrive_y(test, zb)
        waiting = fresh
    lax.fori_loop(1, n_group, lambda i, _: a_copy(i).start(), None)
    for test, zb in waiting:
        arrive_y(test, zb)
    for i in range(1, n_seq):
        other = lax.rem(seq - i + n_seq, n_seq)
        for e in range(n_expert):
            landed(None, every.at[other * n_expert + e], cr.at[i, e])
    for i in range(1, n_dp):
        landed(None, weights.at[lax.rem(dp - i + n_dp, n_dp)], wr.at[i])

    def finish(i, _):
        landed(None, names.at[lax.rem(me - i + n_group, n_group)], rr.at[i])
        r_copy(i).wait_send()
        landed(None, acts.at[lax.rem(me - i + n_group, n_group)], ra.at[i])
        a_copy(i).wait_send()

    lax.fori_loop(1, n_group, finish, None)
    for test, make in sends:
        when(test, lambda make=make: make().wait_send())
    for one in locals_:
        one.wait()


def gather(out_grad, weight, named, packed):
    n_dp, n_seq, n_expert = (lax.axis_size(name) for name in ("dp", "seq", "expert"))
    minor = 1 << ((n_expert.bit_length() - 1) // 2)
    lines = n_expert // minor
    sems = pltpu.SemaphoreType.DMA
    hbm = pl.BlockSpec(memory_space=pl.ANY)
    return pl.pallas_call(
        functools.partial(gather_kernel, (n_dp, n_seq, n_expert, minor)),
        out_shape=(
            jax.ShapeDtypeStruct((n_seq * n_expert,) + out_grad.shape, out_grad.dtype),
            jax.ShapeDtypeStruct((n_dp,) + weight.shape, weight.dtype),
            jax.ShapeDtypeStruct((n_seq * n_expert,) + named.shape, named.dtype),
            jax.ShapeDtypeStruct(packed.shape, packed.dtype),
        ),
        in_specs=[hbm] * 4,
        out_specs=(hbm,) * 4,
        scratch_shapes=[
            sems((4,)),
            sems((2, lines)),
            sems((2, lines)),
            sems((2, minor, lines)),
            sems((2, minor, lines)),
            sems((n_seq, n_expert)),
            sems((n_seq, n_expert)),
            sems((n_dp,)),
            sems((n_dp,)),
            sems((n_seq * n_expert,)),
            sems((n_seq * n_expert,)),
            sems((n_seq * n_expert,)),
            sems((n_seq * n_expert,)),
        ],
        compiler_params=pltpu.CompilerParams(collective_id=0, has_side_effects=True),
        name="gather",
    )(out_grad, weight, named, packed)


def local(out_grad, saved_act, gate_probs, routes, w_down):
    tokens, top = routes.shape
    hidden = saved_act.shape[2]
    features = out_grad.shape[1]
    owners = lax.axis_size(GROUP)
    pairs = tokens * top
    most = max(2, min(tokens, pairs // owners + pairs // (8 * owners)))
    rows = -(-most // 8) * 8
    tall = rows * 2 // 3
    folds = rows % 16 != 0 and rows % 24 == 0 and tall % 16 == 0 and hidden % 256 == 0
    if not folds:
        rows = -(-rows // 16) * 16
    capacity = owners * rows
    f32, bf16 = jnp.float32, jnp.bfloat16


    ids = jnp.arange(owners, dtype=jnp.int32)
    named = routes[:, :, None] == ids[None, None, :]
    names = jnp.any(named, axis=1)
    before = (jnp.arange(tokens)[:, None] > jnp.arange(tokens)[None, :]).astype(bf16)
    rank = jnp.dot(before, names.astype(bf16), preferred_element_type=f32)
    rank_of = jnp.sum(jnp.where(named, rank[:, None, :], 0.0), axis=2).astype(jnp.int32)
    slot = (routes * rows + rank_of).reshape(pairs)
    place = (slot[:, None] == jnp.arange(capacity, dtype=jnp.int32)[None, :]).astype(bf16)

    act = saved_act.reshape(pairs, hidden)
    gate = gate_probs.reshape(pairs, 1)
    scaled = (act.astype(f32) * gate).astype(bf16)
    packed = lax.dot_general(
        place, scaled, (((0,), (0,)), ((), ())), preferred_element_type=f32
    ).astype(bf16)
    packed = packed.reshape(owners, rows, hidden)
    half, rest = hidden // 2, rows - tall
    if folds:
        low = packed[:, tall:]
        low = jnp.concatenate([low[:, :, :half], low[:, :, half:]], axis=1)
        packed = jnp.concatenate([packed[:, :tall], low], axis=2)
    grads_all, weight, routes_all, recv_act = gather(out_grad, w_down[0], routes.T, packed)
    weight = weight.reshape(-1, features)
    if folds:
        low = recv_act[:, :, hidden:]
        low = jnp.concatenate([low[:, :rest], low[:, rest:]], axis=2)
        recv_act = jnp.concatenate([recv_act[:, :, :hidden], low], axis=1)
    recv_act = recv_act.reshape(capacity, hidden)

    mine = lax.axis_index(GROUP)
    has = jnp.any(routes_all == mine, axis=1)
    rank_all = jnp.dot(has.astype(bf16), before.T, preferred_element_type=f32).astype(jnp.int32)
    pick = (
        has[:, None, :]
        & (rank_all[:, None, :] == jnp.arange(rows, dtype=jnp.int32)[None, :, None])
    ).astype(bf16)
    chosen = (
        lax.dot_general(pick, grads_all, (((2,), (1,)), ((0,), (0,))), preferred_element_type=f32)
        .astype(bf16)
        .reshape(capacity, features)
    )
    grad = lax.dot_general(
        chosen, weight, (((1,), (1,)), ((), ())), preferred_element_type=f32
    ).astype(bf16)
    back = lax.all_to_all(
        grad.reshape(owners, rows, hidden), GROUP, split_axis=0, concat_axis=0, tiled=True
    ).reshape(capacity, hidden)
    recv_act, _ = lax.optimization_barrier((recv_act, grad))
    part = lax.dot_general(
        recv_act, chosen, (((0,), (0,)), ((), ())), preferred_element_type=f32
    ).astype(bf16)
    weight_grad = lax.psum_scatter(part, "dp", scatter_dimension=0, tiled=True).reshape(
        w_down.shape
    )
    home = jnp.dot(place, back, preferred_element_type=f32)
    act_grad = (home * gate).astype(bf16).reshape(saved_act.shape)
    prob_grad = jnp.sum(home * act.astype(f32), axis=1).reshape(routes.shape)
    return act_grad, prob_grad, weight_grad


def solution(mesh):
    in_specs = (
        P(("dp", "seq", "expert"), None),
        P(("dp", "seq", "expert"), None, None),
        P(("dp", "seq", "expert"), None),
        P(("dp", "seq", "expert"), None),
        P(("seq", "expert"), "dp", None),
    )
    out_specs = (
        P(("dp", "seq", "expert"), None, None),
        P(("dp", "seq", "expert"), None),
        P(("seq", "expert"), "dp", None),
    )
    return jax.shard_map(local, mesh=mesh, in_specs=in_specs, out_specs=out_specs, check_vma=False)
```

```python
import functools

import jax
import jax.numpy as jnp
from jax import lax
from jax.experimental import pallas as pl
from jax.experimental.pallas import tpu as pltpu
from jax.sharding import PartitionSpec as P

GROUP = ("seq", "expert")


def both(*tests):
    result = tests[0]
    for test in tests[1:]:
        result = jnp.logical_and(result, test)
    return result


def gather_kernel(
    sizes, own, weight, named, packed, every, weights, names, acts,
    here, zs, zr, ys, yr, cs, cr, ws, wr, rs, rr, sa, ra
):
    n_dp, n_seq, n_expert, minor = sizes
    lines = n_expert // minor
    dp, seq, expert = lax.axis_index("dp"), lax.axis_index("seq"), lax.axis_index("expert")
    z, y = expert // minor, expert % minor

    def inside(value, size):
        return both(value >= 0, value < size)

    n_group = n_seq * n_expert
    me = seq * n_expert + expert
    barrier = pltpu.get_barrier_semaphore()

    def member(i):
        index = lax.rem(me + i, n_group)
        return (dp, index // n_expert, lax.rem(index, n_expert))

    def greet(device):
        pl.semaphore_signal(
            barrier, inc=1, device_id=device, device_id_type=pl.DeviceIdType.MESH
        )

    lax.fori_loop(1, n_group, lambda i, _: greet(member(i)), None)
    for i in range(1, n_dp):
        greet((lax.rem(dp + i, n_dp), seq, expert))
    pl.semaphore_wait(barrier, n_group + n_dp - 2)

    def when(test, body):
        if test is None:
            body()
        else:
            pl.when(test)(body)

    sends = []

    def copy(source, target, send, recv, device):
        return pltpu.make_async_remote_copy(
            src_ref=source,
            dst_ref=target,
            send_sem=send,
            recv_sem=recv,
            device_id=device,
            device_id_type=pl.DeviceIdType.MESH,
        )

    def start(test, make):
        when(test, lambda: make().start())
        sends.append((test, make))

    def place(zb, yb):
        return seq * n_expert + zb * minor + yb

    def block(zb, yb, is_own):
        return own if is_own else every.at[place(zb, yb)]

    def z_copy(way, hop):
        zb = z - way * (hop - 1)
        return copy(
            block(zb, y, hop == 1),
            every.at[place(zb, y)],
            zs.at[(1 - way) // 2, hop],
            zr.at[(1 - way) // 2, hop],
            (dp, seq, expert + way * minor),
        )

    def y_copy(way, hop, zb, is_own):
        yb = y - way * (hop - 1)
        return copy(
            block(zb, yb, is_own and hop == 1),
            every.at[place(zb, yb)],
            ys.at[(1 - way) // 2, hop, zb],
            yr.at[(1 - way) // 2, hop, zb],
            (dp, seq, expert + way),
        )

    def c_copy(i, zb, yb, is_own):
        return copy(
            block(zb, yb, is_own),
            every.at[place(zb, yb)],
            cs.at[i, zb * minor + yb],
            cr.at[i, zb * minor + yb],
            (dp, lax.rem(seq + i, n_seq), expert),
        )

    def w_copy(i):
        return copy(
            weight, weights.at[dp], ws.at[i], wr.at[i], (lax.rem(dp + i, n_dp), seq, expert)
        )

    def landed(test, ref, sem):
        when(test, lambda: copy(ref, ref, sem, sem, (dp, seq, expert)).wait_recv())

    def to_cores(test, zb, yb, is_own):
        for i in range(1, n_seq):
            start(test, functools.partial(c_copy, i, zb, yb, is_own))

    def spread(test, zb, is_own):
        for way in (1, -1):
            go = inside(y + way, minor)
            go = go if test is None else both(test, go)
            start(go, functools.partial(y_copy, way, 1, zb, is_own))
        to_cores(test, zb, y, is_own)

    def arrive_y(test, zb):
        for hop in range(1, minor):
            for way in (1, -1):
                yb = y - way * hop
                got = inside(yb, minor)
                got = got if test is None else both(test, got)
                landed(got, every.at[place(zb, yb)], yr.at[(1 - way) // 2, hop, zb])
                if hop + 1 < minor:
                    start(
                        both(got, inside(y + way, minor)),
                        functools.partial(y_copy, way, hop + 1, zb, False),
                    )
                to_cores(got, zb, yb, False)

    def r_copy(i):
        return copy(named, names.at[me], rs.at[i], rr.at[i], member(i))

    def a_copy(i):
        index = lax.rem(me + i, n_group)
        return copy(packed.at[index], acts.at[me], sa.at[i], ra.at[i], member(i))

    for way in (1, -1):
        start(inside(z + way, lines), functools.partial(z_copy, way, 1))
    spread(None, z, True)
    for i in range(1, n_dp):
        start(None, functools.partial(w_copy, i))
    lax.fori_loop(1, n_group, lambda i, _: r_copy(i).start(), None)
    locals_ = [
        pltpu.make_async_copy(named, names.at[me], here.at[2]),
        pltpu.make_async_copy(packed.at[me], acts.at[me], here.at[3]),
        pltpu.make_async_copy(own, every.at[place(z, y)], here.at[0]),
        pltpu.make_async_copy(weight, weights.at[dp], here.at[1]),
    ]
    for one in locals_:
        one.start()
    waiting = [(None, z)]
    for hop in range(1, lines):
        fresh = []
        for way in (1, -1):
            zb = z - way * hop
            got = inside(zb, lines)
            landed(got, every.at[place(zb, y)], zr.at[(1 - way) // 2, hop])
            if hop + 1 < lines:
                start(both(got, inside(z + way, lines)), functools.partial(z_copy, way, hop + 1))
            spread(got, zb, False)
            fresh.append((got, zb))
        for test, zb in waiting:
            arrive_y(test, zb)
        waiting = fresh
    lax.fori_loop(1, n_group, lambda i, _: a_copy(i).start(), None)
    for test, zb in waiting:
        arrive_y(test, zb)
    for i in range(1, n_seq):
        other = lax.rem(seq - i + n_seq, n_seq)
        for e in range(n_expert):
            landed(None, every.at[other * n_expert + e], cr.at[i, e])
    for i in range(1, n_dp):
        landed(None, weights.at[lax.rem(dp - i + n_dp, n_dp)], wr.at[i])

    def finish(i, _):
        landed(None, names.at[lax.rem(me - i + n_group, n_group)], rr.at[i])
        r_copy(i).wait_send()
        landed(None, acts.at[lax.rem(me - i + n_group, n_group)], ra.at[i])
        a_copy(i).wait_send()

    lax.fori_loop(1, n_group, finish, None)
    for test, make in sends:
        when(test, lambda make=make: make().wait_send())
    for one in locals_:
        one.wait()


def gather(out_grad, weight, named, packed):
    n_dp, n_seq, n_expert = (lax.axis_size(name) for name in ("dp", "seq", "expert"))
    minor = 1 << ((n_expert.bit_length() - 1) // 2)
    lines = n_expert // minor
    sems = pltpu.SemaphoreType.DMA
    hbm = pl.BlockSpec(memory_space=pl.ANY)
    return pl.pallas_call(
        functools.partial(gather_kernel, (n_dp, n_seq, n_expert, minor)),
        out_shape=(
            jax.ShapeDtypeStruct((n_seq * n_expert,) + out_grad.shape, out_grad.dtype),
            jax.ShapeDtypeStruct((n_dp,) + weight.shape, weight.dtype),
            jax.ShapeDtypeStruct((n_seq * n_expert,) + named.shape, named.dtype),
            jax.ShapeDtypeStruct(packed.shape, packed.dtype),
        ),
        in_specs=[hbm] * 4,
        out_specs=(hbm,) * 4,
        scratch_shapes=[
            sems((4,)),
            sems((2, lines)),
            sems((2, lines)),
            sems((2, minor, lines)),
            sems((2, minor, lines)),
            sems((n_seq, n_expert)),
            sems((n_seq, n_expert)),
            sems((n_dp,)),
            sems((n_dp,)),
            sems((n_seq * n_expert,)),
            sems((n_seq * n_expert,)),
            sems((n_seq * n_expert,)),
            sems((n_seq * n_expert,)),
        ],
        compiler_params=pltpu.CompilerParams(collective_id=0, has_side_effects=True),
        name="gather",
    )(out_grad, weight, named, packed)


def exchange_kernel(sizes, blocks, arrived, here, send, recv):
    n_seq, n_expert = sizes
    n_group = n_seq * n_expert
    dp, seq, expert = lax.axis_index("dp"), lax.axis_index("seq"), lax.axis_index("expert")
    me = seq * n_expert + expert
    barrier = pltpu.get_barrier_semaphore()

    def member(i):
        index = lax.rem(me + i, n_group)
        return (dp, index // n_expert, lax.rem(index, n_expert))

    def greet(i, _):
        pl.semaphore_signal(
            barrier, inc=1, device_id=member(i), device_id_type=pl.DeviceIdType.MESH
        )

    def push(source, target, i):
        return pltpu.make_async_remote_copy(
            src_ref=source,
            dst_ref=target,
            send_sem=send.at[i],
            recv_sem=recv.at[i],
            device_id=member(i),
            device_id_type=pl.DeviceIdType.MESH,
        )

    def out(i):
        return push(blocks.at[lax.rem(me + i, n_group)], arrived.at[me], i)

    def finish(i, _):
        block = arrived.at[lax.rem(me - i + n_group, n_group)]
        push(block, block, i).wait_recv()
        out(i).wait_send()

    lax.fori_loop(1, n_group, greet, None)
    pl.semaphore_wait(barrier, n_group - 1)
    lax.fori_loop(1, n_group, lambda i, _: out(i).start(), None)
    kept = pltpu.make_async_copy(blocks.at[me], arrived.at[me], here.at[0])
    kept.start()
    lax.fori_loop(1, n_group, finish, None)
    kept.wait()


def exchange(blocks):
    n_seq, n_expert = lax.axis_size("seq"), lax.axis_size("expert")
    sems = pltpu.SemaphoreType.DMA
    hbm = pl.BlockSpec(memory_space=pl.ANY)
    return pl.pallas_call(
        functools.partial(exchange_kernel, (n_seq, n_expert)),
        out_shape=jax.ShapeDtypeStruct(blocks.shape, blocks.dtype),
        in_specs=[hbm],
        out_specs=hbm,
        scratch_shapes=[sems((1,)), sems((n_seq * n_expert,)), sems((n_seq * n_expert,))],
        compiler_params=pltpu.CompilerParams(collective_id=1, has_side_effects=True),
        name="exchange",
    )(blocks)


def local(out_grad, saved_act, gate_probs, routes, w_down):
    tokens, top = routes.shape
    hidden = saved_act.shape[2]
    features = out_grad.shape[1]
    owners = lax.axis_size(GROUP)
    pairs = tokens * top
    most = max(2, min(tokens, pairs // owners + pairs // (8 * owners)))
    rows = -(-most // 8) * 8
    tall = rows * 2 // 3
    folds = rows % 16 != 0 and rows % 24 == 0 and tall % 16 == 0 and hidden % 256 == 0
    if not folds:
        rows = -(-rows // 16) * 16
    capacity = owners * rows
    f32, bf16 = jnp.float32, jnp.bfloat16


    ids = jnp.arange(owners, dtype=jnp.int32)
    named = routes[:, :, None] == ids[None, None, :]
    names = jnp.any(named, axis=1)
    before = (jnp.arange(tokens)[:, None] > jnp.arange(tokens)[None, :]).astype(bf16)
    rank = jnp.dot(before, names.astype(bf16), preferred_element_type=f32)
    rank_of = jnp.sum(jnp.where(named, rank[:, None, :], 0.0), axis=2).astype(jnp.int32)
    slot = (routes * rows + rank_of).reshape(pairs)
    place = (slot[:, None] == jnp.arange(capacity, dtype=jnp.int32)[None, :]).astype(bf16)

    act = saved_act.reshape(pairs, hidden)
    gate = gate_probs.reshape(pairs, 1)
    scaled = (act.astype(f32) * gate).astype(bf16)
    packed = lax.dot_general(
        place, scaled, (((0,), (0,)), ((), ())), preferred_element_type=f32
    ).astype(bf16)
    half, rest = hidden // 2, rows - tall

    def fold(array):
        array = array.reshape(owners, rows, hidden)
        if not folds:
            return array
        low = array[:, tall:]
        low = jnp.concatenate([low[:, :, :half], low[:, :, half:]], axis=1)
        return jnp.concatenate([array[:, :tall], low], axis=2)

    def unfold(array):
        if folds:
            low = array[:, :, hidden:]
            low = jnp.concatenate([low[:, :rest], low[:, rest:]], axis=2)
            array = jnp.concatenate([array[:, :, :hidden], low], axis=1)
        return array.reshape(capacity, hidden)

    grads_all, weight, routes_all, recv_act = gather(
        out_grad, w_down[0], routes.T, fold(packed)
    )
    weight = weight.reshape(-1, features)
    recv_act = unfold(recv_act)

    mine = lax.axis_index(GROUP)
    has = jnp.any(routes_all == mine, axis=1)
    rank_all = jnp.dot(has.astype(bf16), before.T, preferred_element_type=f32).astype(jnp.int32)
    pick = (
        has[:, None, :]
        & (rank_all[:, None, :] == jnp.arange(rows, dtype=jnp.int32)[None, :, None])
    ).astype(bf16)
    chosen = (
        lax.dot_general(pick, grads_all, (((2,), (1,)), ((0,), (0,))), preferred_element_type=f32)
        .astype(bf16)
        .reshape(capacity, features)
    )
    grad = lax.dot_general(
        chosen, weight, (((1,), (1,)), ((), ())), preferred_element_type=f32
    ).astype(bf16)
    part = lax.dot_general(
        recv_act, chosen, (((0,), (0,)), ((), ())), preferred_element_type=f32
    ).astype(bf16)
    grad, part = lax.optimization_barrier((grad, part))
    back = unfold(exchange(fold(grad)))
    weight_grad = lax.psum_scatter(part, "dp", scatter_dimension=0, tiled=True).reshape(
        w_down.shape
    )
    home = jnp.dot(place, back, preferred_element_type=f32)
    act_grad = (home * gate).astype(bf16).reshape(saved_act.shape)
    prob_grad = jnp.sum(home * act.astype(f32), axis=1).reshape(routes.shape)
    return act_grad, prob_grad, weight_grad


def solution(mesh):
    in_specs = (
        P(("dp", "seq", "expert"), None),
        P(("dp", "seq", "expert"), None, None),
        P(("dp", "seq", "expert"), None),
        P(("dp", "seq", "expert"), None),
        P(("seq", "expert"), "dp", None),
    )
    out_specs = (
        P(("dp", "seq", "expert"), None, None),
        P(("dp", "seq", "expert"), None),
        P(("seq", "expert"), "dp", None),
    )
    return jax.shard_map(local, mesh=mesh, in_specs=in_specs, out_specs=out_specs, check_vma=False)
```

```python
import functools

import jax
import jax.numpy as jnp
from jax import lax
from jax.experimental import pallas as pl
from jax.experimental.pallas import tpu as pltpu
from jax.sharding import PartitionSpec as P

GROUP = ("seq", "expert")


def both(*tests):
    result = tests[0]
    for test in tests[1:]:
        result = jnp.logical_and(result, test)
    return result


def gather_kernel(
    sizes, own, weight, named, packed, every, weights, names, acts,
    here, zs, zr, ys, yr, cs, cr, ws, wr, rs, rr, sa, ra
):
    n_dp, n_seq, n_expert, minor = sizes
    lines = n_expert // minor
    dp, seq, expert = lax.axis_index("dp"), lax.axis_index("seq"), lax.axis_index("expert")
    z, y = expert // minor, expert % minor

    def inside(value, size):
        return both(value >= 0, value < size)

    n_group = n_seq * n_expert
    me = seq * n_expert + expert
    barrier = pltpu.get_barrier_semaphore()

    def member(i):
        index = lax.rem(me + i, n_group)
        return (dp, index // n_expert, lax.rem(index, n_expert))

    def greet(device):
        pl.semaphore_signal(
            barrier, inc=1, device_id=device, device_id_type=pl.DeviceIdType.MESH
        )

    lax.fori_loop(1, n_group, lambda i, _: greet(member(i)), None)
    for i in range(1, n_dp):
        greet((lax.rem(dp + i, n_dp), seq, expert))
    pl.semaphore_wait(barrier, n_group + n_dp - 2)

    def when(test, body):
        if test is None:
            body()
        else:
            pl.when(test)(body)

    sends = []

    def copy(source, target, send, recv, device):
        return pltpu.make_async_remote_copy(
            src_ref=source,
            dst_ref=target,
            send_sem=send,
            recv_sem=recv,
            device_id=device,
            device_id_type=pl.DeviceIdType.MESH,
        )

    def start(test, make):
        when(test, lambda: make().start())
        sends.append((test, make))

    def place(zb, yb):
        return seq * n_expert + zb * minor + yb

    def block(zb, yb, is_own):
        return own if is_own else every.at[place(zb, yb)]

    def z_copy(way, hop):
        zb = z - way * (hop - 1)
        return copy(
            block(zb, y, hop == 1),
            every.at[place(zb, y)],
            zs.at[(1 - way) // 2, hop],
            zr.at[(1 - way) // 2, hop],
            (dp, seq, expert + way * minor),
        )

    def y_copy(way, hop, zb, is_own):
        yb = y - way * (hop - 1)
        return copy(
            block(zb, yb, is_own and hop == 1),
            every.at[place(zb, yb)],
            ys.at[(1 - way) // 2, hop, zb],
            yr.at[(1 - way) // 2, hop, zb],
            (dp, seq, expert + way),
        )

    def c_copy(i, zb, yb, is_own):
        return copy(
            block(zb, yb, is_own),
            every.at[place(zb, yb)],
            cs.at[i, zb * minor + yb],
            cr.at[i, zb * minor + yb],
            (dp, lax.rem(seq + i, n_seq), expert),
        )

    def w_copy(i):
        return copy(
            weight, weights.at[dp], ws.at[i], wr.at[i], (lax.rem(dp + i, n_dp), seq, expert)
        )

    def landed(test, ref, sem):
        when(test, lambda: copy(ref, ref, sem, sem, (dp, seq, expert)).wait_recv())

    def to_cores(test, zb, yb, is_own):
        for i in range(1, n_seq):
            start(test, functools.partial(c_copy, i, zb, yb, is_own))

    def spread(test, zb, is_own):
        for way in (1, -1):
            go = inside(y + way, minor)
            go = go if test is None else both(test, go)
            start(go, functools.partial(y_copy, way, 1, zb, is_own))
        to_cores(test, zb, y, is_own)

    def arrive_y(test, zb):
        for hop in range(1, minor):
            for way in (1, -1):
                yb = y - way * hop
                got = inside(yb, minor)
                got = got if test is None else both(test, got)
                landed(got, every.at[place(zb, yb)], yr.at[(1 - way) // 2, hop, zb])
                if hop + 1 < minor:
                    start(
                        both(got, inside(y + way, minor)),
                        functools.partial(y_copy, way, hop + 1, zb, False),
                    )
                to_cores(got, zb, yb, False)

    def r_copy(i):
        return copy(named, names.at[me], rs.at[i], rr.at[i], member(i))

    def a_copy(i):
        index = lax.rem(me + i, n_group)
        return copy(packed.at[index], acts.at[me], sa.at[i], ra.at[i], member(i))

    for way in (1, -1):
        start(inside(z + way, lines), functools.partial(z_copy, way, 1))
    spread(None, z, True)
    for i in range(1, n_dp):
        start(None, functools.partial(w_copy, i))
    lax.fori_loop(1, n_group, lambda i, _: r_copy(i).start(), None)
    locals_ = [
        pltpu.make_async_copy(named, names.at[me], here.at[2]),
        pltpu.make_async_copy(packed.at[me], acts.at[me], here.at[3]),
        pltpu.make_async_copy(own, every.at[place(z, y)], here.at[0]),
        pltpu.make_async_copy(weight, weights.at[dp], here.at[1]),
    ]
    for one in locals_:
        one.start()
    waiting = [(None, z)]
    for hop in range(1, lines):
        fresh = []
        for way in (1, -1):
            zb = z - way * hop
            got = inside(zb, lines)
            landed(got, every.at[place(zb, y)], zr.at[(1 - way) // 2, hop])
            if hop + 1 < lines:
                start(both(got, inside(z + way, lines)), functools.partial(z_copy, way, hop + 1))
            spread(got, zb, False)
            fresh.append((got, zb))
        for test, zb in waiting:
            arrive_y(test, zb)
        waiting = fresh
        if hop == max(1, lines - 2):
            lax.fori_loop(1, n_group, lambda i, _: a_copy(i).start(), None)
    for test, zb in waiting:
        arrive_y(test, zb)
    for i in range(1, n_seq):
        other = lax.rem(seq - i + n_seq, n_seq)
        for e in range(n_expert):
            landed(None, every.at[other * n_expert + e], cr.at[i, e])
    for i in range(1, n_dp):
        landed(None, weights.at[lax.rem(dp - i + n_dp, n_dp)], wr.at[i])

    def finish(i, _):
        landed(None, names.at[lax.rem(me - i + n_group, n_group)], rr.at[i])
        r_copy(i).wait_send()
        landed(None, acts.at[lax.rem(me - i + n_group, n_group)], ra.at[i])
        a_copy(i).wait_send()

    lax.fori_loop(1, n_group, finish, None)
    for test, make in sends:
        when(test, lambda make=make: make().wait_send())
    for one in locals_:
        one.wait()


def gather(out_grad, weight, named, packed):
    n_dp, n_seq, n_expert = (lax.axis_size(name) for name in ("dp", "seq", "expert"))
    minor = 1 << ((n_expert.bit_length() - 1) // 2)
    lines = n_expert // minor
    sems = pltpu.SemaphoreType.DMA
    hbm = pl.BlockSpec(memory_space=pl.ANY)
    return pl.pallas_call(
        functools.partial(gather_kernel, (n_dp, n_seq, n_expert, minor)),
        out_shape=(
            jax.ShapeDtypeStruct((n_seq * n_expert,) + out_grad.shape, out_grad.dtype),
            jax.ShapeDtypeStruct((n_dp,) + weight.shape, weight.dtype),
            jax.ShapeDtypeStruct((n_seq * n_expert,) + named.shape, named.dtype),
            jax.ShapeDtypeStruct(packed.shape, packed.dtype),
        ),
        in_specs=[hbm] * 4,
        out_specs=(hbm,) * 4,
        scratch_shapes=[
            sems((4,)),
            sems((2, lines)),
            sems((2, lines)),
            sems((2, minor, lines)),
            sems((2, minor, lines)),
            sems((n_seq, n_expert)),
            sems((n_seq, n_expert)),
            sems((n_dp,)),
            sems((n_dp,)),
            sems((n_seq * n_expert,)),
            sems((n_seq * n_expert,)),
            sems((n_seq * n_expert,)),
            sems((n_seq * n_expert,)),
        ],
        compiler_params=pltpu.CompilerParams(collective_id=0, has_side_effects=True),
        name="gather",
    )(out_grad, weight, named, packed)


def exchange_kernel(sizes, blocks, arrived, here, send, recv):
    n_seq, n_expert = sizes
    n_group = n_seq * n_expert
    dp, seq, expert = lax.axis_index("dp"), lax.axis_index("seq"), lax.axis_index("expert")
    me = seq * n_expert + expert
    barrier = pltpu.get_barrier_semaphore()

    def member(i):
        index = lax.rem(me + i, n_group)
        return (dp, index // n_expert, lax.rem(index, n_expert))

    def greet(i, _):
        pl.semaphore_signal(
            barrier, inc=1, device_id=member(i), device_id_type=pl.DeviceIdType.MESH
        )

    def push(source, target, i):
        return pltpu.make_async_remote_copy(
            src_ref=source,
            dst_ref=target,
            send_sem=send.at[i],
            recv_sem=recv.at[i],
            device_id=member(i),
            device_id_type=pl.DeviceIdType.MESH,
        )

    def out(i):
        return push(blocks.at[lax.rem(me + i, n_group)], arrived.at[me], i)

    def finish(i, _):
        block = arrived.at[lax.rem(me - i + n_group, n_group)]
        push(block, block, i).wait_recv()
        out(i).wait_send()

    lax.fori_loop(1, n_group, greet, None)
    pl.semaphore_wait(barrier, n_group - 1)
    lax.fori_loop(1, n_group, lambda i, _: out(i).start(), None)
    kept = pltpu.make_async_copy(blocks.at[me], arrived.at[me], here.at[0])
    kept.start()
    lax.fori_loop(1, n_group, finish, None)
    kept.wait()


def exchange(blocks):
    n_seq, n_expert = lax.axis_size("seq"), lax.axis_size("expert")
    sems = pltpu.SemaphoreType.DMA
    hbm = pl.BlockSpec(memory_space=pl.ANY)
    return pl.pallas_call(
        functools.partial(exchange_kernel, (n_seq, n_expert)),
        out_shape=jax.ShapeDtypeStruct(blocks.shape, blocks.dtype),
        in_specs=[hbm],
        out_specs=hbm,
        scratch_shapes=[sems((1,)), sems((n_seq * n_expert,)), sems((n_seq * n_expert,))],
        compiler_params=pltpu.CompilerParams(collective_id=1, has_side_effects=True),
        name="exchange",
    )(blocks)


def local(out_grad, saved_act, gate_probs, routes, w_down):
    tokens, top = routes.shape
    hidden = saved_act.shape[2]
    features = out_grad.shape[1]
    owners = lax.axis_size(GROUP)
    pairs = tokens * top
    most = max(2, min(tokens, pairs // owners + pairs // (8 * owners)))
    rows = -(-most // 8) * 8
    tall = rows * 2 // 3
    folds = rows % 16 != 0 and rows % 24 == 0 and tall % 16 == 0 and hidden % 256 == 0
    if not folds:
        rows = -(-rows // 16) * 16
    capacity = owners * rows
    f32, bf16 = jnp.float32, jnp.bfloat16


    ids = jnp.arange(owners, dtype=jnp.int32)
    named = routes[:, :, None] == ids[None, None, :]
    names = jnp.any(named, axis=1)
    before = (jnp.arange(tokens)[:, None] > jnp.arange(tokens)[None, :]).astype(bf16)
    rank = jnp.dot(before, names.astype(bf16), preferred_element_type=f32)
    rank_of = jnp.sum(jnp.where(named, rank[:, None, :], 0.0), axis=2).astype(jnp.int32)
    slot = (routes * rows + rank_of).reshape(pairs)
    place = (slot[:, None] == jnp.arange(capacity, dtype=jnp.int32)[None, :]).astype(bf16)

    act = saved_act.reshape(pairs, hidden)
    gate = gate_probs.reshape(pairs, 1)
    scaled = (act.astype(f32) * gate).astype(bf16)
    packed = lax.dot_general(
        place, scaled, (((0,), (0,)), ((), ())), preferred_element_type=f32
    ).astype(bf16)
    half, rest = hidden // 2, rows - tall

    def fold(array):
        array = array.reshape(owners, rows, hidden)
        if not folds:
            return array
        low = array[:, tall:]
        low = jnp.concatenate([low[:, :, :half], low[:, :, half:]], axis=1)
        return jnp.concatenate([array[:, :tall], low], axis=2)

    def unfold(array):
        if folds:
            low = array[:, :, hidden:]
            low = jnp.concatenate([low[:, :rest], low[:, rest:]], axis=2)
            array = jnp.concatenate([array[:, :, :hidden], low], axis=1)
        return array.reshape(capacity, hidden)

    grads_all, weight, routes_all, recv_act = gather(
        out_grad, w_down[0], routes.T, fold(packed)
    )
    weight = weight.reshape(-1, features)
    recv_act = unfold(recv_act)

    mine = lax.axis_index(GROUP)
    has = jnp.any(routes_all == mine, axis=1)
    rank_all = jnp.dot(has.astype(bf16), before.T, preferred_element_type=f32).astype(jnp.int32)
    pick = (
        has[:, None, :]
        & (rank_all[:, None, :] == jnp.arange(rows, dtype=jnp.int32)[None, :, None])
    ).astype(bf16)
    chosen = (
        lax.dot_general(pick, grads_all, (((2,), (1,)), ((0,), (0,))), preferred_element_type=f32)
        .astype(bf16)
        .reshape(capacity, features)
    )
    grad = lax.dot_general(
        chosen, weight, (((1,), (1,)), ((), ())), preferred_element_type=f32
    ).astype(bf16)
    part = lax.dot_general(
        recv_act, chosen, (((0,), (0,)), ((), ())), preferred_element_type=f32
    ).astype(bf16)
    grad, part = lax.optimization_barrier((grad, part))
    back = unfold(exchange(fold(grad)))
    weight_grad = lax.psum_scatter(part, "dp", scatter_dimension=0, tiled=True).reshape(
        w_down.shape
    )
    home = jnp.dot(place, back, preferred_element_type=f32)
    act_grad = (home * gate).astype(bf16).reshape(saved_act.shape)
    prob_grad = jnp.sum(home * act.astype(f32), axis=1).reshape(routes.shape)
    return act_grad, prob_grad, weight_grad


def solution(mesh):
    in_specs = (
        P(("dp", "seq", "expert"), None),
        P(("dp", "seq", "expert"), None, None),
        P(("dp", "seq", "expert"), None),
        P(("dp", "seq", "expert"), None),
        P(("seq", "expert"), "dp", None),
    )
    out_specs = (
        P(("dp", "seq", "expert"), None, None),
        P(("dp", "seq", "expert"), None),
        P(("seq", "expert"), "dp", None),
    )
    return jax.shard_map(local, mesh=mesh, in_specs=in_specs, out_specs=out_specs, check_vma=False)
```
